32 devices in a mesh: groups: 2 (over x), fit: 16 (over z, y, core).
Axes of the slice: x: 2, y: 2, z: 4, core: 2. Of those that a mesh axis runs over, the one named last changes fastest.
Arguments:
- three_center: bfloat16 [32, 16, 128, 128], P(('groups', 'fit')), parts along dimension 0, may hold values from -2 to 2
- pair_ids: int32 [32, 16], P(('groups', 'fit')), parts along dimension 0, may hold values from 0 to 63, as said below
- col_tiles: int32 [32, 4], P('groups'), parts along dimension 0, may hold values from 0 to 15, as said below
- orbitals: bfloat16 [4096, 256], P('groups'), parts along dimension 0, may hold values from -0.5 to 0.5
- metric_root: bfloat16 [32, 16], P(('groups', 'fit')), parts along dimension 0
Outputs:
- exchange_matrix: float32 [4096, 512], P(('groups', 'fit')), parts along dimension 0
The draws below stay inside these ranges and needn't reach their ends.
There are 2 independent parts, one for each index of `groups`. The reference program is written for one: setup_inputs(seed, part) draws one part's arguments, and reference() takes and returns one part's arrays. A program takes and returns all parts, laid end to end along the dimension named above; each array names one. Nothing has to cross between parts.
Inputs may be any that keep to these rules, and one draw needn't show every extreme that they name: `col_tiles`: each row tile a lists 4 distinct tiles, the first being a itself. `pair_ids`: each fitting block lists 16 distinct pairs.
All inputs are finite; a program needn't handle non-finite values.
Results may differ from the reference program's by a relative error of at most 0.005.
Values may be sent and summed in bfloat16 or wider, within the bound.
A program may use at most 64 MiB of HBM per device.

```python
import math
import jax
import jax.numpy as jnp
from jax import lax

TB = 128
NOCC = 256
NT = 16
NNZR = 4
NZ = 16
PF_DEV = 1
NB = 2048
NPAIR = 64
NFIT = 16
N_FIT = 16


def draw_col_tiles(key, part):
    key = jax.random.fold_in(key, 11)
    scores = jax.random.randint(key, (NT, NT), 0, 1 << 16) * NT + jnp.arange(NT, dtype=jnp.int32)[None, :]
    scores = scores.at[:, 0].set(-1)
    offsets = jnp.argsort(scores, axis=1)[:, :NNZR]
    return ((jnp.arange(NT, dtype=jnp.int32)[:, None] + offsets) % NT).astype(jnp.int32)


def draw_pair_ids(key, part):
    key = jax.random.fold_in(key, 23)
    scores = jax.random.randint(key, (N_FIT, NPAIR), 0, 1 << 16) * NPAIR + jnp.arange(NPAIR, dtype=jnp.int32)[None, :]
    return jnp.argsort(scores, axis=1)[:, :NZ].astype(jnp.int32)


def draw_metric_root(key, part):
    key = jax.random.fold_in(key, 37)
    first, second = jax.random.split(key)
    noise = jax.random.normal(first, (NFIT, NFIT), jnp.float32)
    noise = noise * (0.35 / math.sqrt(NFIT))
    diagonal = jax.random.uniform(second, (NFIT,), jnp.float32, 0.5, 1.5)
    identity = (jnp.arange(NFIT)[:, None] == jnp.arange(NFIT)[None, :]).astype(jnp.float32)
    return (noise + noise.T + identity * diagonal[:, None]).astype(jnp.bfloat16)


def block_scale(rng, extent, pieces, least, top_value):
    def one(dim, shards_of):
        steps = jax.random.uniform(jax.random.fold_in(jax.random.fold_in(rng, 6), dim), (shards_of,), jnp.float32, least / len(pieces), top_value / len(pieces))
        return jnp.repeat(jnp.exp(steps), extent[dim] // shards_of).reshape((-1,) + (1,) * (len(extent) - dim - 1))

    gain = one(*pieces[0])
    for cut in pieces[1:]:
        gain = gain * one(*cut)
    return gain


def scatter_about(own_key, extent, deviation, limit, shards=(), kind=jnp.bfloat16):
    entries = jax.random.normal(own_key, extent, jnp.float32) * deviation
    if len(shards) > 0:
        entries = block_scale(own_key, extent, shards, -0.22, 0.18) * entries
    return jnp.clip(entries, min=-limit, max=limit).astype(kind)


def setup_inputs(seed: int = 0, part: int = 0) -> dict:
    key_list = jax.random.split(jax.random.key(seed), 6)
    part_splits = jax.random.split(jax.random.fold_in(key_list[5], part), 6)
    return {
        "three_center": scatter_about(part_splits[0], (NFIT, NZ, TB, TB), (max(1, NFIT * NOCC // 512)) ** -0.5, 2.0, ((0, 16),)),
        "pair_ids": draw_pair_ids(jax.random.fold_in(jax.random.fold_in(key_list[5], part), 71), part),
        "col_tiles": draw_col_tiles(jax.random.fold_in(jax.random.fold_in(key_list[5], part), 71), part),
        "orbitals": scatter_about(part_splits[3], (NB, NOCC), TB ** -0.5, 0.5),
        "metric_root": draw_metric_root(jax.random.fold_in(jax.random.fold_in(key_list[5], part), 71), part),
    }


def reference(three_center, pair_ids, col_tiles, orbitals, metric_root):
    orbital_tiles = orbitals.reshape(NT, TB, NOCC)
    row_tiles = pair_ids // NNZR
    column_tiles = col_tiles[row_tiles, pair_ids % NNZR]
    blocks = three_center.reshape(N_FIT, PF_DEV, NZ, TB, TB)

    def half_block(packed):
        tile_block, row_ids, col_ids = packed
        picked = orbital_tiles[col_ids].astype(jnp.float32)
        partial_value = jnp.einsum('psmn,sni->psmi', tile_block.astype(jnp.float32), picked)
        onehot = (row_ids[:, None] == jnp.arange(NT, dtype=jnp.int32)[None, :]).astype(jnp.float32)
        return jnp.einsum('psmi,sa->apmi', partial_value, onehot).astype(jnp.bfloat16)

    half_blocks = lax.map(half_block, (blocks, row_tiles, column_tiles))
    half_blocks = jnp.moveaxis(half_blocks, 0, 1).reshape(NT, NFIT, TB, NOCC)
    metric = metric_root.astype(jnp.float32)

    def fit_tile(tile_block):
        return jnp.einsum('pq,qmi->pmi', metric, tile_block.astype(jnp.float32)).astype(jnp.bfloat16)

    fitted = lax.map(fit_tile, half_blocks)

    def pair_tile(packed):
        own_tile, col_list = packed
        others = fitted[col_list].astype(jnp.float32)
        return jnp.einsum('pmi,rpni->mrn', own_tile.astype(jnp.float32), others)

    exchange_matrix = lax.map(pair_tile, (fitted, col_tiles))
    return exchange_matrix.reshape(NB, NNZR * TB)
```

```python
import functools

import jax
import jax.numpy as jnp
from jax import lax
from jax.experimental import pallas as pl
from jax.experimental.pallas import tpu as pltpu
from jax.sharding import PartitionSpec as P

MESH = pl.DeviceIdType.MESH
Y_COUNT = 2
CORES = 2


def general(three_center, pair_ids, col_tiles, orbitals, metric_root):
    blocks_dev = three_center.shape[0]
    tile_rows = three_center.shape[2]
    tile_count = col_tiles.shape[0]
    per_row = col_tiles.shape[1]
    basis_size = orbitals.shape[0]
    occupied = orbitals.shape[1]
    orbital_tiles = orbitals.reshape(tile_count, tile_rows, occupied)
    slot_ids = pair_ids[0]
    row_tiles = slot_ids // per_row
    column_tiles = col_tiles[row_tiles, slot_ids % per_row]
    picked = jnp.take(orbital_tiles, column_tiles, axis=0)
    partial_value = jnp.einsum(
        "psmn,sni->psmi", three_center, picked, preferred_element_type=jnp.float32
    )
    onehot = (row_tiles[:, None] == jnp.arange(tile_count, dtype=jnp.int32)[None, :]).astype(
        jnp.float32
    )
    metric_full = lax.all_gather(metric_root, "fit", axis=0, tiled=True)
    summands = []
    half_blocks = jnp.einsum("psmi,sa->pami", partial_value, onehot).astype(jnp.bfloat16)
    half_blocks = half_blocks.reshape(blocks_dev, basis_size, occupied)
    spread = lax.all_to_all(half_blocks, "fit", split_axis=1, concat_axis=0, tiled=True)
    fitted = jnp.einsum(
        "pq,qmi->pmi", metric_full, spread, preferred_element_type=jnp.float32
    ).astype(jnp.bfloat16)
    owned_rows = lax.all_to_all(fitted, "fit", split_axis=0, concat_axis=1, tiled=True)
    owned_rows = owned_rows.reshape(blocks_dev, tile_count, tile_rows, occupied)
    for column in range(per_row):
        others = jnp.take(owned_rows, col_tiles[:, column], axis=1)
        summands.append(
            jnp.einsum("pami,pani->amn", owned_rows, others, preferred_element_type=jnp.float32)
        )
    partial_k = jnp.stack(summands, axis=2).reshape(basis_size, per_row * tile_rows)
    return lax.psum_scatter(partial_k, "fit", scatter_dimension=0, tiled=True)


def kernel(
    n, per_row, tb,
    slot_ref, has_ref, col_ref, three_ref, orb_ref, kron_ref, out_ref,
    orb_t, send_h, recv_h, fit_n, fit_t, send_c, recv_c, acc, send_y, recv_y, send_z, recv_z,
    own_sem, sh_sem, rh_sem, sc_sem, rc_sem, sy_sem, ry_sem, sz_sem, rz_sem,
):
    tiles = orb_ref.shape[0] // tb
    basis = tiles * tb
    occ = orb_ref.shape[1]
    depth = occ // n
    z_count = n // (Y_COUNT * CORES)
    me = lax.axis_index("fit")
    core = lax.rem(me, CORES)
    y = lax.rem(me // CORES, Y_COUNT)
    z = me // (CORES * Y_COUNT)

    def at(dz, dy, dc):
        zz = lax.rem(z + dz, z_count)
        yy = lax.rem(y + dy, Y_COUNT)
        cc = lax.rem(core + dc, CORES)
        return (zz * Y_COUNT + yy) * CORES + cc

    offsets = [
        (dz, dy, dc)
        for dz in (2, 1, 3, 0)
        for dy in range(Y_COUNT)
        for dc in range(CORES)
        if (dz, dy, dc) != (0, 0, 0)
    ]
    barrier = pltpu.get_barrier_semaphore()
    for off in offsets:
        pl.semaphore_signal(barrier, inc=1, device_id={"fit": at(*off)}, device_id_type=MESH)

    def turn(b, carry):
        rows = pl.ds(pl.multiple_of(b * tb, tb), tb)
        orb_t[b] = orb_ref[rows, :].T
        return carry

    lax.fori_loop(0, tiles, turn, 0)
    for d in range(n):
        send_h[d * depth:(d + 1) * depth, basis:] = kron_ref[...]

    for a in range(tiles):
        total = jnp.zeros((occ, tb), jnp.float32)
        for r in range(per_row):
            q = a * per_row + r
            block = three_ref[slot_ref[q]]
            block = jnp.where(has_ref[q] > 0, block, jnp.zeros_like(block))
            total += lax.dot_general(
                orb_t[col_ref[q]], block, (((1,), (1,)), ((), ())),
                preferred_element_type=jnp.float32,
            )
        send_h[:, a * tb:(a + 1) * tb] = total.astype(jnp.bfloat16)

    pl.semaphore_wait(barrier, n - 1)

    def rows_of(d):
        return pl.ds(pl.multiple_of(d * depth, depth), depth)

    copies = []
    for k, off in enumerate(offsets):
        dst = at(*off)
        copy = pltpu.make_async_remote_copy(
            src_ref=send_h.at[rows_of(dst), :],
            dst_ref=recv_h.at[rows_of(me), :],
            send_sem=sh_sem.at[k],
            recv_sem=rh_sem.at[k],
            device_id={"fit": dst},
            device_id_type=MESH,
        )
        copy.start()
        copies.append(copy)
    own = pltpu.make_async_copy(send_h.at[rows_of(me), :], recv_h.at[rows_of(me), :], own_sem)
    own.start()
    own.wait()
    for copy in copies:
        copy.wait_recv()

    kron = recv_h[:, basis:]
    for a in range(tiles):
        value = jnp.dot(
            kron, recv_h[:, a * tb:(a + 1) * tb], preferred_element_type=jnp.float32
        ).astype(jnp.bfloat16)
        fit_n[a] = value
        fit_t[a] = value.T

    half_tiles = tiles // CORES
    quarter = half_tiles // Y_COUNT

    def part(a, r):
        return jnp.dot(
            fit_t[a], fit_n[col_ref[a * per_row + r]], preferred_element_type=jnp.float32
        )

    pending = list(copies)
    core_copies = []
    for r in range(per_row):

        def one(j, carry, r=r):
            send_c[r, j] = part(j * CORES + (1 - core), r).astype(jnp.bfloat16)
            return carry

        lax.fori_loop(0, half_tiles, one, 0)
        copy = pltpu.make_async_remote_copy(
            src_ref=send_c.at[r], dst_ref=recv_c.at[r],
            send_sem=sc_sem.at[r], recv_sem=rc_sem.at[r],
            device_id={"fit": at(0, 0, 1)}, device_id_type=MESH,
        )
        copy.start()
        core_copies.append(copy)
    y_copies = []
    for r in range(per_row):
        core_copies[r].wait_recv()

        def theirs(j, carry, r=r):
            t = j * Y_COUNT + (1 - y)
            value = part(t * CORES + core, r) + recv_c[r, t].astype(jnp.float32)
            send_y[r, j] = value.astype(jnp.bfloat16)
            return carry

        lax.fori_loop(0, quarter, theirs, 0)
        copy = pltpu.make_async_remote_copy(
            src_ref=send_y.at[r], dst_ref=recv_y.at[r],
            send_sem=sy_sem.at[r], recv_sem=ry_sem.at[r],
            device_id={"fit": at(0, 1, 0)}, device_id_type=MESH,
        )
        copy.start()
        y_copies.append(copy)

        def mine(j, carry, r=r):
            t = j * Y_COUNT + y
            acc[r, j] = part(t * CORES + core, r) + recv_c[r, t].astype(jnp.float32)
            return carry

        lax.fori_loop(0, quarter, mine, 0)
    z_copies = []
    for r in range(per_row):
        y_copies[r].wait_recv()
        row = []
        for k, dz in enumerate((2, 1, 3)):
            zz = lax.rem(z + dz, z_count)
            send_z[r, k] = (acc[r, zz] + recv_y[r, zz].astype(jnp.float32)).astype(jnp.bfloat16)
            copy = pltpu.make_async_remote_copy(
                src_ref=send_z.at[r, k], dst_ref=recv_z.at[r, k],
                send_sem=sz_sem.at[r, k], recv_sem=rz_sem.at[r, k],
                device_id={"fit": at(dz, 0, 0)}, device_id_type=MESH,
            )
            copy.start()
            row.append(copy)
        z_copies.append(row)
    for r in range(per_row):
        value = acc[r, z] + recv_y[r, z].astype(jnp.float32)
        for k in range(z_count - 1):
            z_copies[r][k].wait_recv()
            value += recv_z[r, k].astype(jnp.float32)
        out_ref[:, r * tb:(r + 1) * tb] = value
    for copy in pending + core_copies + y_copies + [c for row in z_copies for c in row]:
        copy.wait_send()


def fused(n, three_center, pair_ids, col_tiles, orbitals, metric_root):
    tiles, per_row = col_tiles.shape
    slots, tb = three_center.shape[1:3]
    basis, occ = orbitals.shape
    depth = occ // n
    pairs = tiles * per_row
    match = pair_ids[0][None, :] == jnp.arange(pairs, dtype=jnp.int32)[:, None]
    has = jnp.any(match, axis=1).astype(jnp.int32)
    slot = jnp.sum(jnp.where(match, jnp.arange(slots, dtype=jnp.int32)[None, :], 0), axis=1)
    lane = jnp.arange(n * depth, dtype=jnp.int32)
    spread = jnp.repeat(metric_root[0], depth)
    kron = jnp.where(
        (lane % depth)[None, :] == jnp.arange(depth, dtype=jnp.int32)[:, None], spread[None, :], 0
    ).astype(jnp.bfloat16)
    z_count = n // (Y_COUNT * CORES)
    half_tiles = tiles // CORES
    bf = jnp.bfloat16
    dma = pltpu.SemaphoreType.DMA
    vmem = pl.BlockSpec(memory_space=pltpu.VMEM)
    smem = pl.BlockSpec(memory_space=pltpu.SMEM)
    return pl.pallas_call(
        functools.partial(kernel, n, per_row, tb),
        out_shape=jax.ShapeDtypeStruct((tb, per_row * tb), jnp.float32),
        in_specs=[smem, smem, smem, vmem, vmem, vmem],
        out_specs=vmem,
        scratch_shapes=[
            pltpu.VMEM((tiles, occ, tb), bf),
            pltpu.VMEM((occ, basis + occ), bf),
            pltpu.VMEM((occ, basis + occ), bf),
            pltpu.VMEM((tiles, occ, tb), bf),
            pltpu.VMEM((tiles, tb, occ), bf),
            pltpu.VMEM((per_row, half_tiles, tb, tb), bf),
            pltpu.VMEM((per_row, half_tiles, tb, tb), bf),
            pltpu.VMEM((per_row, z_count, tb, tb), jnp.float32),
            pltpu.VMEM((per_row, z_count, tb, tb), bf),
            pltpu.VMEM((per_row, z_count, tb, tb), bf),
            pltpu.VMEM((per_row, z_count - 1, tb, tb), bf),
            pltpu.VMEM((per_row, z_count - 1, tb, tb), bf),
            dma, dma((n - 1,)), dma((n - 1,)),
            dma((per_row,)), dma((per_row,)), dma((per_row,)), dma((per_row,)),
            dma((per_row, z_count - 1)), dma((per_row, z_count - 1)),
        ],
        compiler_params=pltpu.CompilerParams(
            collective_id=0, has_side_effects=True, vmem_limit_bytes=48 * 1024 * 1024
        ),
    )(slot, has, col_tiles.reshape(-1), three_center[0], orbitals, kron)


def solution(mesh):
    in_specs = (
        P(("groups", "fit"), None, None, None),
        P(("groups", "fit"), None),
        P("groups", None),
        P("groups", None),
        P(("groups", "fit"), None),
    )
    out_specs = P(("groups", "fit"), None)
    n = mesh.shape["fit"]

    def local(three_center, pair_ids, col_tiles, orbitals, metric_root):
        args = (three_center, pair_ids, col_tiles, orbitals, metric_root)
        fits = (
            n == 16
            and col_tiles.shape[0] == n
            and three_center.shape[0] == 1
            and orbitals.shape[1] == 16 * n
        )
        return fused(n, *args) if fits else general(*args)

    return jax.shard_map(local, mesh=mesh, in_specs=in_specs, out_specs=out_specs, check_vma=False)
```

```python
import functools

import jax
import jax.numpy as jnp
from jax import lax
from jax.experimental import pallas as pl
from jax.experimental.pallas import tpu as pltpu
from jax.sharding import PartitionSpec as P

MESH = pl.DeviceIdType.MESH
Y_COUNT = 2
CORES = 2
CHUNKS = 4


def general(three_center, pair_ids, col_tiles, orbitals, metric_root):
    blocks_dev = three_center.shape[0]
    tile_rows = three_center.shape[2]
    tile_count = col_tiles.shape[0]
    per_row = col_tiles.shape[1]
    basis_size = orbitals.shape[0]
    occupied = orbitals.shape[1]
    orbital_tiles = orbitals.reshape(tile_count, tile_rows, occupied)
    slot_ids = pair_ids[0]
    row_tiles = slot_ids // per_row
    column_tiles = col_tiles[row_tiles, slot_ids % per_row]
    picked = jnp.take(orbital_tiles, column_tiles, axis=0)
    partial_value = jnp.einsum(
        "psmn,sni->psmi", three_center, picked, preferred_element_type=jnp.float32
    )
    onehot = (row_tiles[:, None] == jnp.arange(tile_count, dtype=jnp.int32)[None, :]).astype(
        jnp.float32
    )
    metric_full = lax.all_gather(metric_root, "fit", axis=0, tiled=True)
    summands = []
    half_blocks = jnp.einsum("psmi,sa->pami", partial_value, onehot).astype(jnp.bfloat16)
    half_blocks = half_blocks.reshape(blocks_dev, basis_size, occupied)
    spread = lax.all_to_all(half_blocks, "fit", split_axis=1, concat_axis=0, tiled=True)
    fitted = jnp.einsum(
        "pq,qmi->pmi", metric_full, spread, preferred_element_type=jnp.float32
    ).astype(jnp.bfloat16)
    owned_rows = lax.all_to_all(fitted, "fit", split_axis=0, concat_axis=1, tiled=True)
    owned_rows = owned_rows.reshape(blocks_dev, tile_count, tile_rows, occupied)
    for column in range(per_row):
        others = jnp.take(owned_rows, col_tiles[:, column], axis=1)
        summands.append(
            jnp.einsum("pami,pani->amn", owned_rows, others, preferred_element_type=jnp.float32)
        )
    partial_k = jnp.stack(summands, axis=2).reshape(basis_size, per_row * tile_rows)
    return lax.psum_scatter(partial_k, "fit", scatter_dimension=0, tiled=True)


def kernel(
    n, per_row, tb,
    slot_ref, has_ref, col_ref, three_ref, orb_ref, kron_ref, out_ref,
    orb_v, three_v, orb_t, send_h, recv_h, recv_m, fit_n, fit_t, send_c, recv_c, acc, send_y, recv_y, send_z, recv_z,
    in_sem, own_sem, sm_sem, rm_sem, sh_sem, rh_sem, sc_sem, rc_sem, sy_sem, ry_sem, sz_sem, rz_sem,
):
    tiles = orb_ref.shape[0] // tb
    basis = tiles * tb
    chunks = send_h.shape[0]
    chunk_tiles = tiles // chunks
    chunk_rows = basis // chunks
    occ = orb_ref.shape[1]
    depth = occ // n
    z_count = n // (Y_COUNT * CORES)
    me = lax.axis_index("fit")
    core = lax.rem(me, CORES)
    y = lax.rem(me // CORES, Y_COUNT)
    z = me // (CORES * Y_COUNT)

    def at(dz, dy, dc):
        zz = lax.rem(z + dz, z_count)
        yy = lax.rem(y + dy, Y_COUNT)
        cc = lax.rem(core + dc, CORES)
        return (zz * Y_COUNT + yy) * CORES + cc

    loads = [
        pltpu.make_async_copy(
            orb_ref.at[c * chunk_rows:(c + 1) * chunk_rows],
            orb_v.at[c * chunk_rows:(c + 1) * chunk_rows],
            in_sem.at[c],
        )
        for c in range(chunks)
    ]
    loads.append(pltpu.make_async_copy(three_ref, three_v, in_sem.at[chunks]))
    for load in loads:
        load.start()

    offsets = [
        (dz, dy, dc)
        for dz in (2, 1, 3, 0)
        for dy in range(Y_COUNT)
        for dc in range(CORES)
        if (dz, dy, dc) != (0, 0, 0)
    ]
    barrier = pltpu.get_barrier_semaphore()
    for off in offsets:
        pl.semaphore_signal(barrier, inc=1, device_id={"fit": at(*off)}, device_id_type=MESH)

    def rows_of(d):
        return pl.ds(pl.multiple_of(d * depth, depth), depth)

    for b in range(tiles):
        if b % chunk_tiles == 0:
            loads[b // chunk_tiles].wait()
        orb_t[b] = orb_v[b * tb:(b + 1) * tb, :].T
    loads[-1].wait()
    pl.semaphore_wait(barrier, n - 1)

    recv_m[rows_of(me), :] = kron_ref[...]
    metric_copies = []
    for k, off in enumerate(offsets):
        copy = pltpu.make_async_remote_copy(
            src_ref=kron_ref,
            dst_ref=recv_m.at[rows_of(me), :],
            send_sem=sm_sem.at[k],
            recv_sem=rm_sem.at[k],
            device_id={"fit": at(*off)},
            device_id_type=MESH,
        )
        copy.start()
        metric_copies.append(copy)

    copies = []
    for c in range(chunks):
        for t in range(chunk_tiles):
            total = jnp.zeros((occ, tb), jnp.float32)
            for r in range(per_row):
                q = (c * chunk_tiles + t) * per_row + r
                block = three_v[slot_ref[q]]
                block = jnp.where(has_ref[q] > 0, block, jnp.zeros_like(block))
                total += lax.dot_general(
                    orb_t[col_ref[q]], block, (((1,), (1,)), ((), ())),
                    preferred_element_type=jnp.float32,
                )
            send_h[c, :, t * tb:(t + 1) * tb] = total.astype(jnp.bfloat16)
        row = []
        for k, off in enumerate(offsets):
            dst = at(*off)
            copy = pltpu.make_async_remote_copy(
                src_ref=send_h.at[c, rows_of(dst), :],
                dst_ref=recv_h.at[c, rows_of(me), :],
                send_sem=sh_sem.at[c, k],
                recv_sem=rh_sem.at[c, k],
                device_id={"fit": dst},
                device_id_type=MESH,
            )
            copy.start()
            row.append(copy)
        copies.append(row)
    owns = []
    for c in range(chunks):
        own = pltpu.make_async_copy(
            send_h.at[c, rows_of(me), :], recv_h.at[c, rows_of(me), :], own_sem.at[c]
        )
        own.start()
        owns.append(own)
    for copy in metric_copies:
        copy.wait_recv()
    kron = recv_m[...]

    for c in range(chunks):
        owns[c].wait()
        for copy in copies[c]:
            copy.wait_recv()
        for t in range(chunk_tiles):
            value = jnp.dot(
                kron, recv_h[c, :, t * tb:(t + 1) * tb], preferred_element_type=jnp.float32
            ).astype(jnp.bfloat16)
            fit_n[c * chunk_tiles + t] = value
            fit_t[c * chunk_tiles + t] = value.T

    half_tiles = tiles // CORES
    quarter = half_tiles // Y_COUNT

    def part(a, r):
        return jnp.dot(
            fit_t[a], fit_n[col_ref[a * per_row + r]], preferred_element_type=jnp.float32
        )

    def to_core(r):
        for j in range(half_tiles):
            send_c[r, j] = part(j * CORES + (1 - core), r).astype(jnp.bfloat16)
        copy = pltpu.make_async_remote_copy(
            src_ref=send_c.at[r], dst_ref=recv_c.at[r],
            send_sem=sc_sem.at[r], recv_sem=rc_sem.at[r],
            device_id={"fit": at(0, 0, 1)}, device_id_type=MESH,
        )
        copy.start()
        return copy

    def to_y(r):
        core_copies[r].wait_recv()
        for j in range(quarter):
            t = j * Y_COUNT + (1 - y)
            value = part(t * CORES + core, r) + recv_c[r, t].astype(jnp.float32)
            send_y[r, j] = value.astype(jnp.bfloat16)
        copy = pltpu.make_async_remote_copy(
            src_ref=send_y.at[r], dst_ref=recv_y.at[r],
            send_sem=sy_sem.at[r], recv_sem=ry_sem.at[r],
            device_id={"fit": at(0, 1, 0)}, device_id_type=MESH,
        )
        copy.start()
        return copy

    core_copies = [to_core(0)]
    y_copies = []
    for r in range(1, per_row):
        core_copies.append(to_core(r))
        y_copies.append(to_y(r - 1))
    y_copies.append(to_y(per_row - 1))
    for r in range(per_row):
        for j in range(quarter):
            t = j * Y_COUNT + y
            acc[r, j] = part(t * CORES + core, r) + recv_c[r, t].astype(jnp.float32)
    z_copies = []
    for r in range(per_row):
        y_copies[r].wait_recv()
        row = []
        for k, dz in enumerate((2, 1, 3)):
            zz = lax.rem(z + dz, z_count)
            send_z[r, k] = (acc[r, zz] + recv_y[r, zz].astype(jnp.float32)).astype(jnp.bfloat16)
            copy = pltpu.make_async_remote_copy(
                src_ref=send_z.at[r, k], dst_ref=recv_z.at[r, k],
                send_sem=sz_sem.at[r, k], recv_sem=rz_sem.at[r, k],
                device_id={"fit": at(dz, 0, 0)}, device_id_type=MESH,
            )
            copy.start()
            row.append(copy)
        z_copies.append(row)
    for r in range(per_row):
        value = acc[r, z] + recv_y[r, z].astype(jnp.float32)
        for k in range(z_count - 1):
            z_copies[r][k].wait_recv()
            value += recv_z[r, k].astype(jnp.float32)
        out_ref[:, r * tb:(r + 1) * tb] = value
    started = metric_copies + core_copies + y_copies
    for row in copies + z_copies:
        started += row
    for copy in started:
        copy.wait_send()


def fused(n, three_center, pair_ids, col_tiles, orbitals, metric_root):
    tiles, per_row = col_tiles.shape
    slots, tb = three_center.shape[1:3]
    basis, occ = orbitals.shape
    depth = occ // n
    pairs = tiles * per_row
    match = pair_ids[0][None, :] == jnp.arange(pairs, dtype=jnp.int32)[:, None]
    has = jnp.any(match, axis=1).astype(jnp.int32)
    slot = jnp.sum(jnp.where(match, jnp.arange(slots, dtype=jnp.int32)[None, :], 0), axis=1)
    lane = jnp.arange(n * depth, dtype=jnp.int32)
    spread = jnp.repeat(metric_root[0], depth)
    kron = jnp.where(
        (lane % depth)[None, :] == jnp.arange(depth, dtype=jnp.int32)[:, None], spread[None, :], 0
    ).astype(jnp.bfloat16)
    z_count = n // (Y_COUNT * CORES)
    half_tiles = tiles // CORES
    bf = jnp.bfloat16
    dma = pltpu.SemaphoreType.DMA
    vmem = pl.BlockSpec(memory_space=pltpu.VMEM)
    whole = pl.BlockSpec(memory_space=pl.ANY)
    smem = pl.BlockSpec(memory_space=pltpu.SMEM)
    return pl.pallas_call(
        functools.partial(kernel, n, per_row, tb),
        out_shape=jax.ShapeDtypeStruct((tb, per_row * tb), jnp.float32),
        in_specs=[smem, smem, smem, whole, whole, vmem],
        out_specs=vmem,
        scratch_shapes=[
            pltpu.VMEM((basis, occ), bf),
            pltpu.VMEM((slots, tb, tb), bf),
            pltpu.VMEM((tiles, occ, tb), bf),
            pltpu.VMEM((CHUNKS, occ, basis // CHUNKS), bf),
            pltpu.VMEM((CHUNKS, occ, basis // CHUNKS), bf),
            pltpu.VMEM((occ, occ), bf),
            pltpu.VMEM((tiles, occ, tb), bf),
            pltpu.VMEM((tiles, tb, occ), bf),
            pltpu.VMEM((per_row, half_tiles, tb, tb), bf),
            pltpu.VMEM((per_row, half_tiles, tb, tb), bf),
            pltpu.VMEM((per_row, z_count, tb, tb), jnp.float32),
            pltpu.VMEM((per_row, z_count, tb, tb), bf),
            pltpu.VMEM((per_row, z_count, tb, tb), bf),
            pltpu.VMEM((per_row, z_count - 1, tb, tb), bf),
            pltpu.VMEM((per_row, z_count - 1, tb, tb), bf),
            dma((CHUNKS + 1,)), dma((CHUNKS,)), dma((n - 1,)), dma((n - 1,)),
            dma((CHUNKS, n - 1)), dma((CHUNKS, n - 1)),
            dma((per_row,)), dma((per_row,)), dma((per_row,)), dma((per_row,)),
            dma((per_row, z_count - 1)), dma((per_row, z_count - 1)),
        ],
        compiler_params=pltpu.CompilerParams(
            collective_id=0, has_side_effects=True, vmem_limit_bytes=56 * 1024 * 1024
        ),
    )(slot, has, col_tiles.reshape(-1), three_center[0], orbitals, kron)


def solution(mesh):
    in_specs = (
        P(("groups", "fit"), None, None, None),
        P(("groups", "fit"), None),
        P("groups", None),
        P("groups", None),
        P(("groups", "fit"), None),
    )
    out_specs = P(("groups", "fit"), None)
    n = mesh.shape["fit"]

    def local(three_center, pair_ids, col_tiles, orbitals, metric_root):
        args = (three_center, pair_ids, col_tiles, orbitals, metric_root)
        fits = (
            n == 16
            and col_tiles.shape[0] == n
            and three_center.shape[0] == 1
            and orbitals.shape[1] == 16 * n
        )
        return fused(n, *args) if fits else general(*args)

    return jax.shard_map(local, mesh=mesh, in_specs=in_specs, out_specs=out_specs, check_vma=False)
```

```python
import functools

import jax
import jax.numpy as jnp
from jax import lax
from jax.experimental import pallas as pl
from jax.experimental.pallas import tpu as pltpu
from jax.sharding import PartitionSpec as P

MESH = pl.DeviceIdType.MESH
Y_COUNT = 2
CORES = 2
CHUNKS = 2
HALVES = 2


def general(three_center, pair_ids, col_tiles, orbitals, metric_root):
    blocks_dev = three_center.shape[0]
    tile_rows = three_center.shape[2]
    tile_count = col_tiles.shape[0]
    per_row = col_tiles.shape[1]
    basis_size = orbitals.shape[0]
    occupied = orbitals.shape[1]
    orbital_tiles = orbitals.reshape(tile_count, tile_rows, occupied)
    slot_ids = pair_ids[0]
    row_tiles = slot_ids // per_row
    column_tiles = col_tiles[row_tiles, slot_ids % per_row]
    picked = jnp.take(orbital_tiles, column_tiles, axis=0)
    partial_value = jnp.einsum(
        "psmn,sni->psmi", three_center, picked, preferred_element_type=jnp.float32
    )
    onehot = (row_tiles[:, None] == jnp.arange(tile_count, dtype=jnp.int32)[None, :]).astype(
        jnp.float32
    )
    metric_full = lax.all_gather(metric_root, "fit", axis=0, tiled=True)
    summands = []
    half_blocks = jnp.einsum("psmi,sa->pami", partial_value, onehot).astype(jnp.bfloat16)
    half_blocks = half_blocks.reshape(blocks_dev, basis_size, occupied)
    spread = lax.all_to_all(half_blocks, "fit", split_axis=1, concat_axis=0, tiled=True)
    fitted = jnp.einsum(
        "pq,qmi->pmi", metric_full, spread, preferred_element_type=jnp.float32
    ).astype(jnp.bfloat16)
    owned_rows = lax.all_to_all(fitted, "fit", split_axis=0, concat_axis=1, tiled=True)
    owned_rows = owned_rows.reshape(blocks_dev, tile_count, tile_rows, occupied)
    for column in range(per_row):
        others = jnp.take(owned_rows, col_tiles[:, column], axis=1)
        summands.append(
            jnp.einsum("pami,pani->amn", owned_rows, others, preferred_element_type=jnp.float32)
        )
    partial_k = jnp.stack(summands, axis=2).reshape(basis_size, per_row * tile_rows)
    return lax.psum_scatter(partial_k, "fit", scatter_dimension=0, tiled=True)


def kernel(
    n, per_row, tb,
    ids_ref, col_ref, three_ref, orb_ref, metric_ref, out_ref,
    orb_v, three_v, orb_t, send_h, recv_h, send_m, recv_m, fit_n, fit_t, send_c, recv_c, acc, send_y, recv_y, send_z, recv_z,
    in_sem, own_sem, sm_sem, rm_sem, sh_sem, rh_sem, sc_sem, rc_sem, sy_sem, ry_sem, sz_sem, rz_sem,
):
    tiles = orb_ref.shape[0] // tb
    basis = tiles * tb
    chunks = send_h.shape[0]
    chunk_tiles = tiles // chunks
    chunk_rows = basis // chunks
    occ = orb_ref.shape[1]
    depth = occ // n
    z_count = n // (Y_COUNT * CORES)
    me = lax.axis_index("fit")
    core = lax.rem(me, CORES)
    y = lax.rem(me // CORES, Y_COUNT)
    z = me // (CORES * Y_COUNT)

    def at(dz, dy, dc):
        zz = lax.rem(z + dz, z_count)
        yy = lax.rem(y + dy, Y_COUNT)
        cc = lax.rem(core + dc, CORES)
        return (zz * Y_COUNT + yy) * CORES + cc

    loads = [
        pltpu.make_async_copy(
            orb_ref.at[c * chunk_rows:(c + 1) * chunk_rows],
            orb_v.at[c * chunk_rows:(c + 1) * chunk_rows],
            in_sem.at[c],
        )
        for c in range(chunks)
    ]
    loads.append(pltpu.make_async_copy(three_ref, three_v, in_sem.at[chunks]))
    for load in loads:
        load.start()

    offsets = [
        (dz, dy, dc)
        for dz in (2, 1, 3, 0)
        for dy in range(Y_COUNT)
        for dc in range(CORES)
        if (dz, dy, dc) != (0, 0, 0)
    ]
    barrier = pltpu.get_barrier_semaphore()
    for off in offsets:
        pl.semaphore_signal(barrier, inc=1, device_id={"fit": at(*off)}, device_id_type=MESH)

    def rows_of(d):
        return pl.ds(pl.multiple_of(d * depth, depth), depth)

    for b in range(tiles):
        if b % chunk_tiles == 0:
            loads[b // chunk_tiles].wait()
        orb_t[b] = orb_v[b * tb:(b + 1) * tb, :].T
    loads[-1].wait()
    slots = three_v.shape[0]
    ids = [ids_ref[0, i] for i in range(slots)]

    def send_metric():
        for k, off in enumerate(offsets):
            copy = pltpu.make_async_remote_copy(
                src_ref=send_m,
                dst_ref=recv_m.at[rows_of(me), :],
                send_sem=sm_sem.at[k],
                recv_sem=rm_sem.at[k],
                device_id={"fit": at(*off)},
                device_id_type=MESH,
            )
            copy.start()
            metric_copies.append(copy)

    send_m[...] = jnp.zeros_like(send_m)
    send_m[:, :n] = jnp.broadcast_to(metric_ref[...].astype(jnp.float32), (depth, n)).astype(
        jnp.bfloat16
    )
    recv_m[rows_of(me), :] = send_m[...]
    metric_copies = []

    copies = []
    for c in range(chunks):
        for t in range(chunk_tiles):
            total = jnp.zeros((occ, tb), jnp.float32)
            for r in range(per_row):
                q = (c * chunk_tiles + t) * per_row + r
                slot = jnp.int32(-1)
                for i in range(slots):
                    slot = jnp.where(ids[i] == q, i, slot)
                block = three_v[jnp.maximum(slot, 0)]
                block = jnp.where(slot >= 0, block, jnp.zeros_like(block))
                total += lax.dot_general(
                    orb_t[col_ref[r, c * chunk_tiles + t]], block, (((1,), (1,)), ((), ())),
                    preferred_element_type=jnp.float32,
                )
            send_h[c, :, t * tb:(t + 1) * tb] = total.astype(jnp.bfloat16)
        if c == 0:
            pl.semaphore_wait(barrier, n - 1)
        row = []
        for k, off in enumerate(offsets):
            dst = at(*off)
            copy = pltpu.make_async_remote_copy(
                src_ref=send_h.at[c, rows_of(dst), :],
                dst_ref=recv_h.at[c, rows_of(me), :],
                send_sem=sh_sem.at[c, k],
                recv_sem=rh_sem.at[c, k],
                device_id={"fit": dst},
                device_id_type=MESH,
            )
            copy.start()
            row.append(copy)
        copies.append(row)
        if c == 0:
            send_metric()
    owns = []
    for c in range(chunks):
        own = pltpu.make_async_copy(
            send_h.at[c, rows_of(me), :], recv_h.at[c, rows_of(me), :], own_sem.at[c]
        )
        own.start()
        owns.append(own)
    for copy in metric_copies:
        copy.wait_recv()
    lanes = recv_m.shape[1]
    wide = n * depth
    expand = (
        lax.broadcasted_iota(jnp.int32, (lanes, wide), 1) // depth
        == lax.broadcasted_iota(jnp.int32, (lanes, wide), 0)
    )
    spread = jnp.dot(
        recv_m[...],
        jnp.where(expand, 1.0, 0.0).astype(jnp.bfloat16),
        preferred_element_type=jnp.float32,
    )
    same = (
        lax.broadcasted_iota(jnp.int32, (wide, wide), 1) % depth
        == lax.broadcasted_iota(jnp.int32, (wide, wide), 0) % depth
    )
    kron = jnp.where(same, spread, 0.0).astype(jnp.bfloat16)

    for c in range(chunks):
        owns[c].wait()
        for copy in copies[c]:
            copy.wait_recv()
        for t in range(chunk_tiles):
            value = jnp.dot(
                kron, recv_h[c, :, t * tb:(t + 1) * tb], preferred_element_type=jnp.float32
            ).astype(jnp.bfloat16)
            fit_n[c * chunk_tiles + t] = value
            fit_t[c * chunk_tiles + t] = value.T

    half_tiles = tiles // CORES
    quarter = half_tiles // Y_COUNT

    def part(a, r):
        return jnp.dot(
            fit_t[a], fit_n[col_ref[r, a]], preferred_element_type=jnp.float32
        )

    rows = tb // HALVES

    def to_core(r):
        for j in range(half_tiles):
            send_c[r, j] = part(j * CORES + (1 - core), r).astype(jnp.bfloat16)
        copy = pltpu.make_async_remote_copy(
            src_ref=send_c.at[r], dst_ref=recv_c.at[r],
            send_sem=sc_sem.at[r], recv_sem=rc_sem.at[r],
            device_id={"fit": at(0, 0, 1)}, device_id_type=MESH,
        )
        copy.start()
        return copy

    def to_y(r):
        core_copies[r].wait_recv()
        for j in range(quarter):
            t = j * Y_COUNT + (1 - y)
            value = part(t * CORES + core, r) + recv_c[r, t].astype(jnp.float32)
            for h in range(HALVES):
                send_y[r, h, j] = value[h * rows:(h + 1) * rows].astype(jnp.bfloat16)
        out = []
        for h in range(HALVES):
            copy = pltpu.make_async_remote_copy(
                src_ref=send_y.at[r, h], dst_ref=recv_y.at[r, h],
                send_sem=sy_sem.at[r, h], recv_sem=ry_sem.at[r, h],
                device_id={"fit": at(0, 1, 0)}, device_id_type=MESH,
            )
            copy.start()
            out.append(copy)
        return out

    core_copies = [to_core(0)]
    y_copies = []
    for r in range(1, per_row):
        core_copies.append(to_core(r))
        y_copies.append(to_y(r - 1))
    y_copies.append(to_y(per_row - 1))
    for r in range(per_row):
        for j in range(quarter):
            t = j * Y_COUNT + y
            acc[r, j] = part(t * CORES + core, r) + recv_c[r, t].astype(jnp.float32)
    z_copies = []
    for r in range(per_row):
        for h in range(HALVES):
            span = pl.ds(h * rows, rows)
            y_copies[r][h].wait_recv()
            row = []
            for k, dz in enumerate((2, 1, 3)):
                zz = lax.rem(z + dz, z_count)
                value = acc[r, zz, span, :] + recv_y[r, h, zz].astype(jnp.float32)
                send_z[r, h, k] = value.astype(jnp.bfloat16)
                copy = pltpu.make_async_remote_copy(
                    src_ref=send_z.at[r, h, k], dst_ref=recv_z.at[r, h, k],
                    send_sem=sz_sem.at[r, h, k], recv_sem=rz_sem.at[r, h, k],
                    device_id={"fit": at(dz, 0, 0)}, device_id_type=MESH,
                )
                copy.start()
                row.append(copy)
            z_copies.append(row)
    for r in range(per_row):
        for h in range(HALVES):
            span = pl.ds(h * rows, rows)
            value = acc[r, z, span, :] + recv_y[r, h, z].astype(jnp.float32)
            for k in range(z_count - 1):
                z_copies[r * HALVES + h][k].wait_recv()
                value += recv_z[r, h, k].astype(jnp.float32)
            out_ref[span, r * tb:(r + 1) * tb] = value
    started = metric_copies + core_copies
    for row in copies + y_copies + z_copies:
        started += row
    for copy in started:
        copy.wait_send()


def fused(n, three_center, pair_ids, col_tiles, orbitals, metric_root):
    tiles, per_row = col_tiles.shape
    slots, tb = three_center.shape[1:3]
    basis, occ = orbitals.shape
    depth = occ // n
    z_count = n // (Y_COUNT * CORES)
    half_tiles = tiles // CORES
    bf = jnp.bfloat16
    dma = pltpu.SemaphoreType.DMA
    vmem = pl.BlockSpec(memory_space=pltpu.VMEM)
    whole = pl.BlockSpec(memory_space=pl.ANY)
    smem = pl.BlockSpec(memory_space=pltpu.SMEM)
    return pl.pallas_call(
        functools.partial(kernel, n, per_row, tb),
        out_shape=jax.ShapeDtypeStruct((tb, per_row * tb), jnp.float32),
        in_specs=[smem, smem, whole, whole, vmem],
        out_specs=vmem,
        scratch_shapes=[
            pltpu.VMEM((basis, occ), bf),
            pltpu.VMEM((slots, tb, tb), bf),
            pltpu.VMEM((tiles, occ, tb), bf),
            pltpu.VMEM((CHUNKS, occ, basis // CHUNKS), bf),
            pltpu.VMEM((CHUNKS, occ, basis // CHUNKS), bf),
            pltpu.VMEM((depth, 128), bf),
            pltpu.VMEM((occ, 128), bf),
            pltpu.VMEM((tiles, occ, tb), bf),
            pltpu.VMEM((tiles, tb, occ), bf),
            pltpu.VMEM((per_row, half_tiles, tb, tb), bf),
            pltpu.VMEM((per_row, half_tiles, tb, tb), bf),
            pltpu.VMEM((per_row, z_count, tb, tb), jnp.float32),
            pltpu.VMEM((per_row, HALVES, z_count, tb // HALVES, tb), bf),
            pltpu.VMEM((per_row, HALVES, z_count, tb // HALVES, tb), bf),
            pltpu.VMEM((per_row, HALVES, z_count - 1, tb // HALVES, tb), bf),
            pltpu.VMEM((per_row, HALVES, z_count - 1, tb // HALVES, tb), bf),
            dma((CHUNKS + 1,)), dma((CHUNKS,)), dma((n - 1,)), dma((n - 1,)),
            dma((CHUNKS, n - 1)), dma((CHUNKS, n - 1)),
            dma((per_row,)), dma((per_row,)), dma((per_row, HALVES)), dma((per_row, HALVES)),
            dma((per_row, HALVES, z_count - 1)), dma((per_row, HALVES, z_count - 1)),
        ],
        compiler_params=pltpu.CompilerParams(
            collective_id=0, has_side_effects=True, vmem_limit_bytes=56 * 1024 * 1024
        ),
    )(pair_ids, col_tiles.T, three_center[0], orbitals, metric_root)


def solution(mesh):
    in_specs = (
        P(("groups", "fit"), None, None, None),
        P(("groups", "fit"), None),
        P("groups", None),
        P("groups", None),
        P(("groups", "fit"), None),
    )
    out_specs = P(("groups", "fit"), None)
    n = mesh.shape["fit"]

    def local(three_center, pair_ids, col_tiles, orbitals, metric_root):
        args = (three_center, pair_ids, col_tiles, orbitals, metric_root)
        fits = (
            n == 16
            and col_tiles.shape[0] == n
            and three_center.shape[0] == 1
            and orbitals.shape[1] == 16 * n
        )
        return fused(n, *args) if fits else general(*args)

    return jax.shard_map(local, mesh=mesh, in_specs=in_specs, out_specs=out_specs, check_vma=False)
```

```python
import functools

import jax
import jax.numpy as jnp
from jax import lax
from jax.experimental import pallas as pl
from jax.experimental.pallas import tpu as pltpu
from jax.sharding import PartitionSpec as P

MESH = pl.DeviceIdType.MESH
Y_COUNT = 2
CORES = 2
CHUNKS = 4
HALVES = 2


def general(three_center, pair_ids, col_tiles, orbitals, metric_root):
    blocks_dev = three_center.shape[0]
    tile_rows = three_center.shape[2]
    tile_count = col_tiles.shape[0]
    per_row = col_tiles.shape[1]
    basis_size = orbitals.shape[0]
    occupied = orbitals.shape[1]
    orbital_tiles = orbitals.reshape(tile_count, tile_rows, occupied)
    slot_ids = pair_ids[0]
    row_tiles = slot_ids // per_row
    column_tiles = col_tiles[row_tiles, slot_ids % per_row]
    picked = jnp.take(orbital_tiles, column_tiles, axis=0)
    partial_value = jnp.einsum(
        "psmn,sni->psmi", three_center, picked, preferred_element_type=jnp.float32
    )
    onehot = (row_tiles[:, None] == jnp.arange(tile_count, dtype=jnp.int32)[None, :]).astype(
        jnp.float32
    )
    metric_full = lax.all_gather(metric_root, "fit", axis=0, tiled=True)
    summands = []
    half_blocks = jnp.einsum("psmi,sa->pami", partial_value, onehot).astype(jnp.bfloat16)
    half_blocks = half_blocks.reshape(blocks_dev, basis_size, occupied)
    spread = lax.all_to_all(half_blocks, "fit", split_axis=1, concat_axis=0, tiled=True)
    fitted = jnp.einsum(
        "pq,qmi->pmi", metric_full, spread, preferred_element_type=jnp.float32
    ).astype(jnp.bfloat16)
    owned_rows = lax.all_to_all(fitted, "fit", split_axis=0, concat_axis=1, tiled=True)
    owned_rows = owned_rows.reshape(blocks_dev, tile_count, tile_rows, occupied)
    for column in range(per_row):
        others = jnp.take(owned_rows, col_tiles[:, column], axis=1)
        summands.append(
            jnp.einsum("pami,pani->amn", owned_rows, others, preferred_element_type=jnp.float32)
        )
    partial_k = jnp.stack(summands, axis=2).reshape(basis_size, per_row * tile_rows)
    return lax.psum_scatter(partial_k, "fit", scatter_dimension=0, tiled=True)


def kernel(
    n, per_row, tb,
    ids_ref, col_ref, three_ref, orb_ref, metric_ref, out_ref,
    orb_v, three_v, orb_t, send_h, recv_h, send_m, recv_m, fit_n, fit_t, send_c, recv_c, acc, send_y, recv_y, send_z, recv_z,
    in_sem, own_sem, sm_sem, rm_sem, sh_sem, rh_sem, sc_sem, rc_sem, sy_sem, ry_sem, sz_sem, rz_sem,
):
    tiles = orb_ref.shape[0] // tb
    basis = tiles * tb
    chunks = send_h.shape[0]
    chunk_tiles = tiles // chunks
    chunk_rows = basis // chunks
    occ = orb_ref.shape[1]
    depth = occ // n
    z_count = n // (Y_COUNT * CORES)
    me = lax.axis_index("fit")
    core = lax.rem(me, CORES)
    y = lax.rem(me // CORES, Y_COUNT)
    z = me // (CORES * Y_COUNT)

    def at(dz, dy, dc):
        zz = lax.rem(z + dz, z_count)
        yy = lax.rem(y + dy, Y_COUNT)
        cc = lax.rem(core + dc, CORES)
        return (zz * Y_COUNT + yy) * CORES + cc

    loads = [
        pltpu.make_async_copy(
            orb_ref.at[c * chunk_rows:(c + 1) * chunk_rows],
            orb_v.at[c * chunk_rows:(c + 1) * chunk_rows],
            in_sem.at[c],
        )
        for c in range(chunks)
    ]
    loads.append(pltpu.make_async_copy(three_ref, three_v, in_sem.at[chunks]))
    for load in loads:
        load.start()

    offsets = [
        (dz, dy, dc)
        for dz in (2, 1, 3, 0)
        for dy in range(Y_COUNT)
        for dc in range(CORES)
        if (dz, dy, dc) != (0, 0, 0)
    ]
    barrier = pltpu.get_barrier_semaphore()
    for off in offsets:
        pl.semaphore_signal(barrier, inc=1, device_id={"fit": at(*off)}, device_id_type=MESH)

    def rows_of(d):
        return pl.ds(pl.multiple_of(d * depth, depth), depth)

    for b in range(tiles):
        if b % chunk_tiles == 0:
            loads[b // chunk_tiles].wait()
        orb_t[b] = orb_v[b * tb:(b + 1) * tb, :].T
    loads[-1].wait()
    slots = three_v.shape[0]
    ids = [ids_ref[0, i] for i in range(slots)]

    def send_metric():
        for k, off in enumerate(offsets):
            copy = pltpu.make_async_remote_copy(
                src_ref=send_m,
                dst_ref=recv_m.at[rows_of(me), :],
                send_sem=sm_sem.at[k],
                recv_sem=rm_sem.at[k],
                device_id={"fit": at(*off)},
                device_id_type=MESH,
            )
            copy.start()
            metric_copies.append(copy)

    send_m[...] = jnp.zeros_like(send_m)
    send_m[:, :n] = jnp.broadcast_to(metric_ref[...].astype(jnp.float32), (depth, n)).astype(
        jnp.bfloat16
    )
    recv_m[rows_of(me), :] = send_m[...]
    metric_copies = []

    copies = []
    for c in range(chunks):
        for t in range(chunk_tiles):
            total = jnp.zeros((occ, tb), jnp.float32)
            for r in range(per_row):
                q = (c * chunk_tiles + t) * per_row + r
                slot = jnp.int32(-1)
                for i in range(slots):
                    slot = jnp.where(ids[i] == q, i, slot)
                block = three_v[jnp.maximum(slot, 0)]
                block = jnp.where(slot >= 0, block, jnp.zeros_like(block))
                total += lax.dot_general(
                    orb_t[col_ref[r, c * chunk_tiles + t]], block, (((1,), (1,)), ((), ())),
                    preferred_element_type=jnp.float32,
                )
            send_h[c, :, t * tb:(t + 1) * tb] = total.astype(jnp.bfloat16)
        if c == 0:
            pl.semaphore_wait(barrier, n - 1)
        row = []
        for k, off in enumerate(offsets):
            dst = at(*off)
            copy = pltpu.make_async_remote_copy(
                src_ref=send_h.at[c, rows_of(dst), :],
                dst_ref=recv_h.at[c, rows_of(me), :],
                send_sem=sh_sem.at[c, k],
                recv_sem=rh_sem.at[c, k],
                device_id={"fit": dst},
                device_id_type=MESH,
            )
            copy.start()
            row.append(copy)
        copies.append(row)
        if c == 0:
            send_metric()
    owns = []
    for c in range(chunks):
        own = pltpu.make_async_copy(
            send_h.at[c, rows_of(me), :], recv_h.at[c, rows_of(me), :], own_sem.at[c]
        )
        own.start()
        owns.append(own)
    for copy in metric_copies:
        copy.wait_recv()
    lanes = recv_m.shape[1]
    wide = n * depth
    expand = (
        lax.broadcasted_iota(jnp.int32, (lanes, wide), 1) // depth
        == lax.broadcasted_iota(jnp.int32, (lanes, wide), 0)
    )
    spread = jnp.dot(
        recv_m[...],
        jnp.where(expand, 1.0, 0.0).astype(jnp.bfloat16),
        preferred_element_type=jnp.float32,
    )
    same = (
        lax.broadcasted_iota(jnp.int32, (wide, wide), 1) % depth
        == lax.broadcasted_iota(jnp.int32, (wide, wide), 0) % depth
    )
    kron = jnp.where(same, spread, 0.0).astype(jnp.bfloat16)

    half_tiles = tiles // CORES
    quarter = half_tiles // Y_COUNT

    def part(a, r):
        other = a if r == 0 else col_ref[r, a]
        return jnp.dot(fit_t[a], fit_n[other], preferred_element_type=jnp.float32)

    rows = tb // HALVES

    def to_core(r, c, lo, hi):
        for j in range(lo, hi):
            send_c[r, j] = part(j * CORES + (1 - core), r).astype(jnp.bfloat16)
        copy = pltpu.make_async_remote_copy(
            src_ref=send_c.at[r, lo:hi], dst_ref=recv_c.at[r, lo:hi],
            send_sem=sc_sem.at[r, c], recv_sem=rc_sem.at[r, c],
            device_id={"fit": at(0, 0, 1)}, device_id_type=MESH,
        )
        copy.start()
        return copy

    def to_y(r, c, lo, hi):
        core_copies[r][c].wait_recv()
        for j in range(lo, hi):
            t = j * Y_COUNT + (1 - y)
            value = part(t * CORES + core, r) + recv_c[r, t].astype(jnp.float32)
            for h in range(HALVES):
                send_y[r, h, j] = value[h * rows:(h + 1) * rows].astype(jnp.bfloat16)
        out = []
        for h in range(HALVES):
            copy = pltpu.make_async_remote_copy(
                src_ref=send_y.at[r, h, lo:hi], dst_ref=recv_y.at[r, h, lo:hi],
                send_sem=sy_sem.at[r, c, h], recv_sem=ry_sem.at[r, c, h],
                device_id={"fit": at(0, 1, 0)}, device_id_type=MESH,
            )
            copy.start()
            out.append(copy)
        return out

    core_copies = [[]]
    y_copies = [[]]
    core_step = half_tiles // chunks
    y_step = quarter // chunks

    def first_to_y(c):
        return to_y(0, c, c * y_step, (c + 1) * y_step)

    for c in range(chunks):
        owns[c].wait()
        for copy in copies[c]:
            copy.wait_recv()
        for t in range(chunk_tiles):
            value = jnp.dot(
                kron, recv_h[c, :, t * tb:(t + 1) * tb], preferred_element_type=jnp.float32
            ).astype(jnp.bfloat16)
            fit_n[c * chunk_tiles + t] = value
            fit_t[c * chunk_tiles + t] = value.T
        core_copies[0].append(to_core(0, c, c * core_step, (c + 1) * core_step))
        if c < chunks - 1:
            y_copies[0].append(first_to_y(c))

    for r in range(1, per_row):
        core_copies.append([to_core(r, 0, 0, half_tiles)])
        if r == 1:
            y_copies[0].append(first_to_y(chunks - 1))
        else:
            y_copies.append([to_y(r - 1, 0, 0, quarter)])
    y_copies.append([to_y(per_row - 1, 0, 0, quarter)])
    for r in range(per_row):
        for j in range(quarter):
            t = j * Y_COUNT + y
            acc[r, j] = part(t * CORES + core, r) + recv_c[r, t].astype(jnp.float32)
    z_copies = []
    for r in range(per_row):
        for h in range(HALVES):
            span = pl.ds(h * rows, rows)
            for group in y_copies[r]:
                group[h].wait_recv()
            row = []
            for k, dz in enumerate((2, 1, 3)):
                zz = lax.rem(z + dz, z_count)
                value = acc[r, zz, span, :] + recv_y[r, h, zz].astype(jnp.float32)
                send_z[r, h, k] = value.astype(jnp.bfloat16)
                copy = pltpu.make_async_remote_copy(
                    src_ref=send_z.at[r, h, k], dst_ref=recv_z.at[r, h, k],
                    send_sem=sz_sem.at[r, h, k], recv_sem=rz_sem.at[r, h, k],
                    device_id={"fit": at(dz, 0, 0)}, device_id_type=MESH,
                )
                copy.start()
                row.append(copy)
            z_copies.append(row)
    for r in range(per_row):
        for h in range(HALVES):
            span = pl.ds(h * rows, rows)
            value = acc[r, z, span, :] + recv_y[r, h, z].astype(jnp.float32)
            for k in range(z_count - 1):
                z_copies[r * HALVES + h][k].wait_recv()
                value += recv_z[r, h, k].astype(jnp.float32)
            out_ref[span, r * tb:(r + 1) * tb] = value
    started = list(metric_copies)
    for row in copies + core_copies + z_copies:
        started += row
    for groups in y_copies:
        for group in groups:
            started += group
    for copy in started:
        copy.wait_send()


def fused(n, three_center, pair_ids, col_tiles, orbitals, metric_root):
    tiles, per_row = col_tiles.shape
    slots, tb = three_center.shape[1:3]
    basis, occ = orbitals.shape
    depth = occ // n
    z_count = n // (Y_COUNT * CORES)
    half_tiles = tiles // CORES
    bf = jnp.bfloat16
    dma = pltpu.SemaphoreType.DMA
    vmem = pl.BlockSpec(memory_space=pltpu.VMEM)
    whole = pl.BlockSpec(memory_space=pl.ANY)
    smem = pl.BlockSpec(memory_space=pltpu.SMEM)
    return pl.pallas_call(
        functools.partial(kernel, n, per_row, tb),
        out_shape=jax.ShapeDtypeStruct((tb, per_row * tb), jnp.float32),
        in_specs=[smem, smem, whole, whole, vmem],
        out_specs=vmem,
        scratch_shapes=[
            pltpu.VMEM((basis, occ), bf),
            pltpu.VMEM((slots, tb, tb), bf),
            pltpu.VMEM((tiles, occ, tb), bf),
            pltpu.VMEM((CHUNKS, occ, basis // CHUNKS), bf),
            pltpu.VMEM((CHUNKS, occ, basis // CHUNKS), bf),
            pltpu.VMEM((depth, 128), bf),
            pltpu.VMEM((occ, 128), bf),
            pltpu.VMEM((tiles, occ, tb), bf),
            pltpu.VMEM((tiles, tb, occ), bf),
            pltpu.VMEM((per_row, half_tiles, tb, tb), bf),
            pltpu.VMEM((per_row, half_tiles, tb, tb), bf),
            pltpu.VMEM((per_row, z_count, tb, tb), jnp.float32),
            pltpu.VMEM((per_row, HALVES, z_count, tb // HALVES, tb), bf),
            pltpu.VMEM((per_row, HALVES, z_count, tb // HALVES, tb), bf),
            pltpu.VMEM((per_row, HALVES, z_count - 1, tb // HALVES, tb), bf),
            pltpu.VMEM((per_row, HALVES, z_count - 1, tb // HALVES, tb), bf),
            dma((CHUNKS + 1,)), dma((CHUNKS,)), dma((n - 1,)), dma((n - 1,)),
            dma((CHUNKS, n - 1)), dma((CHUNKS, n - 1)),
            dma((per_row, CHUNKS)), dma((per_row, CHUNKS)),
            dma((per_row, CHUNKS, HALVES)), dma((per_row, CHUNKS, HALVES)),
            dma((per_row, HALVES, z_count - 1)), dma((per_row, HALVES, z_count - 1)),
        ],
        compiler_params=pltpu.CompilerParams(
            collective_id=0, has_side_effects=True, vmem_limit_bytes=56 * 1024 * 1024
        ),
    )(pair_ids, col_tiles.T, three_center[0], orbitals, metric_root)


def solution(mesh):
    in_specs = (
        P(("groups", "fit"), None, None, None),
        P(("groups", "fit"), None),
        P("groups", None),
        P("groups", None),
        P(("groups", "fit"), None),
    )
    out_specs = P(("groups", "fit"), None)
    n = mesh.shape["fit"]

    def local(three_center, pair_ids, col_tiles, orbitals, metric_root):
        args = (three_center, pair_ids, col_tiles, orbitals, metric_root)
        fits = (
            n == 16
            and col_tiles.shape[0] == n
            and three_center.shape[0] == 1
            and orbitals.shape[1] == 16 * n
        )
        return fused(n, *args) if fits else general(*args)

    return jax.shard_map(local, mesh=mesh, in_specs=in_specs, out_specs=out_specs, check_vma=False)
```
